32 devices in a mesh: img: 8 (over z, core), seq: 4 (over y, x).
Axes of the slice: x: 2, y: 2, z: 4, core: 2. Of those that a mesh axis runs over, the one named last changes fastest.
Arguments:
- patches: bfloat16 [8, 4096, 512], P('img', 'seq'), may hold values from -40 to 40
- router: bfloat16 [512, 64], replicated, may hold values from -3 to 3
- w_in: bfloat16 [8, 4096, 512], P('seq', 'img'), may hold values from -0.25 to 0.25
- w_out: bfloat16 [8, 4096, 512], P('seq', 'img'), may hold values from -0.09375 to 0.09375
- cotangent: bfloat16 [8, 4096, 512], P('img', 'seq'), may hold values from -6 to 6
Outputs:
- patch_grad: bfloat16 [8, 4096, 512], P('img', 'seq')
- router_grad: bfloat16 [512, 64], replicated
- w_in_grad: bfloat16 [8, 4096, 512], P('seq', 'img')
- w_out_grad: bfloat16 [8, 4096, 512], P('seq', 'img')
The draws below stay inside these ranges and needn't reach their ends.
All inputs are finite; a program needn't handle non-finite values.
Results may differ from the reference program's by a relative error of at most 0.03.
Values may be sent and summed in bfloat16 or wider, within the bound.
A program may use at most 64 MiB of HBM per device.

```python
import math
import jax
import jax.numpy as jnp
from jax import lax

D = 512
FF = 4096
SLOTS = 8
EXPERTS = 8
PATCHES = 4096
IMAGES = 8


def draw_router(key, part):

    def shared_columns(base_key):
        spread = 3.0 * D ** (-0.5)
        primary = jnp.clip(jax.random.normal(base_key, (D, EXPERTS * SLOTS), jnp.float32), -6.0, 6.0) * spread
        second_key = jax.random.fold_in(base_key, 72)
        spare_half = jnp.clip(jax.random.normal(second_key, (D, EXPERTS * SLOTS), jnp.float32), -6.0, 6.0) * spread
        ordering = jax.random.permutation(jax.random.fold_in(base_key, 71), EXPERTS * SLOTS // 2)
        return (primary, spare_half, ordering[:2])
    primary, spare_half, chosen = shared_columns(key)
    column = jnp.arange(EXPERTS * SLOTS)
    marked = jnp.any((column // 2)[None, :] == chosen[:, None], axis=0)
    odd_column = column % 2 == 1
    lower_half = jnp.arange(D) < D // 2
    partner = jnp.repeat(primary[:, 0::2], 2, axis=1)
    shaped = jnp.where(lower_half[:, None], 1.01 * partner, spare_half)
    return jnp.where((marked & odd_column)[None, :], shaped, primary).astype(jnp.bfloat16)


def draw_patches(key, part):

    def shared_columns(base_key):
        spread = 3.0 * D ** (-0.5)
        primary = jnp.clip(jax.random.normal(base_key, (D, EXPERTS * SLOTS), jnp.float32), -6.0, 6.0) * spread
        second_key = jax.random.fold_in(base_key, 72)
        spare_half = jnp.clip(jax.random.normal(second_key, (D, EXPERTS * SLOTS), jnp.float32), -6.0, 6.0) * spread
        ordering = jax.random.permutation(jax.random.fold_in(base_key, 71), EXPERTS * SLOTS // 2)
        return (primary, spare_half, ordering[:2])

    def first_eight(image_key):
        return jax.random.permutation(image_key, PATCHES)[:8]
    primary, spare_half, chosen = shared_columns(key)
    key = jax.random.fold_in(key, 3)
    subkeys = jax.random.split(key, 5)
    whole_shape = (IMAGES, PATCHES, D)
    jitter = jnp.clip(jax.random.normal(subkeys[0], whole_shape, jnp.float32), -6.0, 6.0)
    ceiling = 240.0
    lower_half = (jnp.arange(D) < D // 2)[:, None]
    first_sign = jnp.where(primary[:, 2 * chosen] >= 0.0, 1.0, -1.0)
    second_sign = jnp.where(spare_half[:, 2 * chosen + 1] >= 0.0, 1.0, -1.0)
    first_dir = jnp.where(lower_half, first_sign, 0.0).T
    second_dir = jnp.where(lower_half, 0.0, second_sign).T
    directions = jnp.stack([first_dir, first_dir, second_dir, second_dir], axis=1).reshape(8, D)
    strength = jax.random.uniform(subkeys[2], (IMAGES, 2), jnp.float32, 110.0, ceiling)
    spacing = jax.random.uniform(subkeys[3], (IMAGES, 2, 2), jnp.float32, 1.0, 3.0)
    levels = jnp.stack([strength, strength + spacing[:, :, 0], 1.2 * strength, 1.2 * strength + spacing[:, :, 1]], axis=2)
    amplitude = levels.reshape(IMAGES, 8) / (1.197 * D ** 0.5)
    planted = amplitude[:, :, None] * directions[None, :, :]
    positions = jax.vmap(first_eight)(jax.random.split(subkeys[4], IMAGES))
    image_ids = jnp.arange(IMAGES)[:, None]
    result = jitter.at[image_ids, positions].multiply(0.15)
    result = result.at[image_ids, positions].add(planted)
    return result.astype(jnp.bfloat16)


def block_levels(key, shape, cuts, low, high):
    gain = 1.0
    for axis_at, blocks in cuts:
        steps = jax.random.uniform(jax.random.fold_in(jax.random.fold_in(key, 6), axis_at), (blocks,), jnp.float32, low / len(cuts), high / len(cuts))
        gain = gain * jnp.repeat(jnp.exp(steps), shape[axis_at] // blocks).reshape((-1,) + (1,) * (len(shape) - 1 - axis_at))
    return gain


def normal_values(rng, extent, deviation, bound, shards=(), held_as=jnp.bfloat16):
    gain = block_levels(rng, extent, shards, -0.22, 0.18) if shards else 1.0
    drawn = jax.random.normal(rng, extent, jnp.float32) * deviation * gain
    return jnp.minimum(jnp.maximum(drawn, -bound), bound).astype(held_as)


def setup_inputs(seed: int = 0) -> dict:
    seeds = jax.random.split(jax.random.key(seed), 6)
    patches = draw_patches(jax.random.fold_in(seeds[5], 71), 0)
    router = draw_router(jax.random.fold_in(seeds[5], 71), 0)
    w_in = normal_values(seeds[2], (EXPERTS, FF, D), D ** -0.5, 0.25, ((0, 4), (1, 8)))
    w_out = normal_values(seeds[3], (EXPERTS, FF, D), FF ** -0.5, 0.09375, ((0, 4), (1, 8)))
    cotangent = normal_values(seeds[4], (IMAGES, PATCHES, D), 1.0, 6.0, ((0, 8), (1, 4)))
    return {"patches": patches, "router": router, "w_in": w_in, "w_out": w_out, "cotangent": cotangent}


def gelu_slope(values):
    coeff = math.sqrt(2.0 / math.pi)
    inside = coeff * (values + 0.044715 * values * values * values)
    tangent = jnp.tanh(inside)
    return 0.5 * (1.0 + tangent) + 0.5 * values * (1.0 - tangent * tangent) * coeff * (1.0 + 3.0 * 0.044715 * values * values)

def weights_of(image_rows, router):
    logits = jnp.dot(image_rows, router, preferred_element_type=jnp.float32)
    highest = lax.optimization_barrier(jnp.max(logits, axis=0, keepdims=True))
    raised = jnp.exp(logits - highest)
    totals = lax.optimization_barrier(jnp.sum(raised, axis=0, keepdims=True))
    dispatch = (raised / totals).astype(jnp.bfloat16)
    combine = jax.nn.softmax(logits, axis=-1).astype(jnp.bfloat16)
    return (dispatch, combine)

def reference(patches, router, w_in, w_out, cotangent):

    def forward_slots(image_rows):
        dispatch, combine = weights_of(image_rows, router)
        return jnp.dot(dispatch.T, image_rows, preferred_element_type=jnp.float32).astype(jnp.bfloat16)
    slot_in = lax.map(forward_slots, patches)
    grouped = slot_in.reshape(IMAGES, EXPERTS, SLOTS, D).astype(jnp.float32)
    hidden = jnp.einsum('besd,efd->besf', grouped, w_in.astype(jnp.float32))
    active = jax.nn.gelu(hidden, approximate=True).astype(jnp.bfloat16)
    slot_out = jnp.einsum('besf,efd->besd', active.astype(jnp.float32), w_out.astype(jnp.float32))
    slot_out = slot_out.astype(jnp.bfloat16).reshape(IMAGES, EXPERTS * SLOTS, D)

    def backward_slots(items):
        image_rows, grad_rows = items
        dispatch, combine = weights_of(image_rows, router)
        return jnp.dot(combine.T, grad_rows, preferred_element_type=jnp.float32).astype(jnp.bfloat16)
    slot_grad = lax.map(backward_slots, (patches, cotangent))
    grad_four = slot_grad.reshape(IMAGES, EXPERTS, SLOTS, D).astype(jnp.float32)
    act_grad = jnp.einsum('besd,efd->besf', grad_four, w_out.astype(jnp.float32))
    hidden_grad = (act_grad * gelu_slope(hidden)).astype(jnp.bfloat16)
    w_out_grad = jnp.einsum('besf,besd->efd', active.astype(jnp.float32), grad_four).astype(jnp.bfloat16)
    w_in_grad = jnp.einsum('besf,besd->efd', hidden_grad.astype(jnp.float32), grouped).astype(jnp.bfloat16)
    input_grad = jnp.einsum('besf,efd->besd', hidden_grad.astype(jnp.float32), w_in.astype(jnp.float32))
    input_grad = input_grad.astype(jnp.bfloat16).reshape(IMAGES, EXPERTS * SLOTS, D)

    def backward_patches(items):
        image_rows, grad_rows, out_rows, in_rows = items
        dispatch, combine = weights_of(image_rows, router)
        comb_grad = jnp.dot(grad_rows, out_rows.T, preferred_element_type=jnp.float32)
        disp_grad = jnp.dot(image_rows, in_rows.T, preferred_element_type=jnp.float32)
        disp_wide = dispatch.astype(jnp.float32)
        comb_wide = combine.astype(jnp.float32)
        inner_sum = lax.optimization_barrier(jnp.sum(disp_wide * disp_grad, axis=0, keepdims=True))
        across = lax.optimization_barrier(jnp.sum(comb_wide * comb_grad, axis=-1, keepdims=True))
        logit_grad = (disp_wide * (disp_grad - inner_sum) + comb_wide * (comb_grad - across)).astype(jnp.bfloat16)
        first_term = jnp.dot(logit_grad, router.T, preferred_element_type=jnp.float32)
        second_term = jnp.dot(dispatch, in_rows, preferred_element_type=jnp.float32)
        patch_rows = (first_term + second_term).astype(jnp.bfloat16)
        router_part = jnp.dot(image_rows.T, logit_grad, preferred_element_type=jnp.float32)
        return (patch_rows, router_part)
    patch_grad, router_parts = lax.map(backward_patches, (patches, cotangent, slot_out, input_grad))
    router_grad = lax.optimization_barrier(jnp.sum(router_parts, axis=0)).astype(jnp.bfloat16)
    return (patch_grad, router_grad, w_in_grad, w_out_grad)
```

```python
import functools
import math

import jax
import jax.numpy as jnp
from jax import lax
from jax.experimental import pallas as pl
from jax.experimental.pallas import tpu as pltpu
from jax.sharding import PartitionSpec as P

SLOTS = 8
MESH = pl.DeviceIdType.MESH
BF = jnp.bfloat16
F32 = jnp.float32
MAX_LANE, TOTAL_LANE, INNER_LANE = 0, 1, 2


def dot(a, b, contract):
    return lax.dot_general(a, b, (contract, ((), ())), preferred_element_type=F32)


def gelu_and_slope(values):
    coeff = math.sqrt(2.0 / math.pi)
    square = values * values
    tangent = jnp.tanh(coeff * values * (1.0 + 0.044715 * square))
    half = 0.5 * (1.0 + tangent)
    slope = half + 0.5 * values * (1.0 - tangent * tangent) * coeff * (1.0 + 3.0 * 0.044715 * square)
    return values * half, slope


class Exchange:
    def __init__(self, axis, count, send_sem, recv_sem):
        self.axis, self.count = axis, count
        self.send_sem, self.recv_sem = send_sem, recv_sem
        self.me = lax.axis_index(axis)
        self.copies = []

    def start(self, source, landing, source_is_own):
        for step in range(1, self.count):
            peer = lax.rem(self.me + step, self.count)
            copy = pltpu.make_async_remote_copy(
                src_ref=source.at[self.me if source_is_own else peer],
                dst_ref=landing.at[self.me],
                send_sem=self.send_sem.at[step],
                recv_sem=self.recv_sem.at[step],
                device_id={self.axis: peer},
                device_id_type=MESH,
            )
            copy.start()
            self.copies.append(copy)

    def wait_recv(self):
        for copy in self.copies:
            copy.wait_recv()

    def wait_send(self):
        for copy in self.copies:
            copy.wait_send()


def kernel(
    n_img, n_seq,
    pat_hbm, rou_hbm, win_hbm, wout_hbm, cot_hbm,
    pg_hbm, rg_hbm, wig_hbm, wog_hbm,
    pat, rou, win, wout, cot,
    pg, rg, wig, wog,
    a_in_s, a_in_r, a_gr_s, a_gr_r, a_st_s, a_st_r,
    b_in, b_gr, c_out_s, c_out_r, c_ig_s, c_ig_r,
    d_out, d_ig, d_st, e_s, e_r, f_buf, g_buf,
    act_s, hg_s,
    load_sem, store_sem, seq_send, seq_recv, img_send, img_recv,
):
    img, seq = lax.axis_index("img"), lax.axis_index("seq")
    experts = win.shape[0]
    rows, depth = b_in.shape[1], b_in.shape[2]
    slots = n_seq * rows

    loads = []
    for at, (src, dst) in enumerate(
        ((pat_hbm.at[0], pat), (rou_hbm, rou), (cot_hbm.at[0], cot), (win_hbm, win), (wout_hbm, wout))
    ):
        copy = pltpu.make_async_copy(src, dst, load_sem.at[at])
        copy.start()
        loads.append(copy)

    barrier = pltpu.get_barrier_semaphore()
    for step in range(1, n_seq):
        pl.semaphore_signal(
            barrier, inc=1, device_id={"seq": lax.rem(seq + step, n_seq)}, device_id_type=MESH
        )
    for step in range(1, n_img):
        pl.semaphore_signal(
            barrier, inc=1, device_id={"img": lax.rem(img + step, n_img)}, device_id_type=MESH
        )

    def over_seq(at):
        return Exchange("seq", n_seq, seq_send.at[at], seq_recv.at[at])

    def over_img(at):
        return Exchange("img", n_img, img_send.at[at], img_recv.at[at])

    started = []

    def go(exchange, source, landing, own):
        exchange.start(source, landing, own)
        started.append(exchange)
        return exchange

    loads[1].wait()
    router_t = rou[...].astype(F32).T.astype(BF)
    loads[0].wait()
    logits = dot(router_t, pat[...], ((1,), (1,)))
    own_max = jnp.max(logits, axis=1, keepdims=True)
    raised = jnp.exp(logits - own_max)
    own_total = jnp.sum(raised, axis=1, keepdims=True)
    part_in = dot((raised * (1.0 / own_total)).astype(BF), pat[...], ((1,), (0,)))
    lane = lax.broadcasted_iota(jnp.int32, (slots, 128), 1)
    a_st_s[...] = jnp.where(lane == MAX_LANE, own_max, own_total).reshape(n_seq, rows, 128)
    a_in_s[...] = part_in.astype(BF).reshape(n_seq, rows, depth)
    a_st_r[seq] = a_st_s[seq]
    a_in_r[seq] = a_in_s[seq]
    pl.semaphore_wait(barrier, n_seq - 1 + n_img - 1)
    a_st = go(over_seq(0), a_st_s, a_st_r, False)
    a_in = go(over_seq(1), a_in_s, a_in_r, False)

    comb = jnp.exp(logits - jnp.max(logits, axis=0, keepdims=True))
    comb = comb * (1.0 / jnp.sum(comb, axis=0, keepdims=True))
    loads[2].wait()
    part_gr = dot(comb.astype(BF), cot[...], ((1,), (0,)))
    a_gr_s[...] = part_gr.astype(BF).reshape(n_seq, rows, depth)
    a_gr_r[seq] = a_gr_s[seq]
    a_gr = go(over_seq(2), a_gr_s, a_gr_r, False)

    a_st.wait_recv()
    a_in.wait_recv()
    stats = a_st_r[...]
    maxes, totals = stats[:, :, MAX_LANE:MAX_LANE + 1], stats[:, :, TOTAL_LANE:TOTAL_LANE + 1]
    top = jnp.max(maxes, axis=0, keepdims=True)
    shares = totals * jnp.exp(maxes - top)
    total = jnp.sum(shares, axis=0, keepdims=True)
    slot_in = jnp.sum(a_in_r[...].astype(F32) * (shares / total), axis=0)
    b_in[img] = slot_in.astype(BF)
    g_in = go(over_img(0), b_in, b_in, True)
    a_gr.wait_recv()
    b_gr[img] = jnp.sum(a_gr_r[...].astype(F32), axis=0).astype(BF)
    g_gr = go(over_img(1), b_gr, b_gr, True)

    def of_expert(buffer, e):
        wide = buffer[...].astype(F32).reshape(n_img, experts, SLOTS, depth)
        return wide[:, e].reshape(n_img * SLOTS, depth).astype(BF)

    def all_rows(parts):
        wide = [part.reshape(n_img, 1, SLOTS, depth) for part in parts]
        return jnp.concatenate(wide, axis=1).reshape(n_img, rows, depth).astype(BF)

    loads[3].wait()
    g_in.wait_recv()
    slopes, parts = [], []
    loads[4].wait()
    for e in range(experts):
        hidden = dot(of_expert(b_in, e), win[e], ((1,), (1,)))
        active, slope = gelu_and_slope(hidden)
        slopes.append(slope)
        act_s[e] = active.astype(BF)
        parts.append(dot(act_s[e], wout[e], ((1,), (0,))))
    c_out_s[...] = all_rows(parts)
    c_out_r[img] = c_out_s[img]
    c_out = go(over_img(2), c_out_s, c_out_r, False)
    g_gr.wait_recv()
    parts = []
    for e in range(experts):
        act_grad = dot(of_expert(b_gr, e), wout[e], ((1,), (1,)))
        hg_s[e] = (act_grad * slopes[e]).astype(BF)
        parts.append(dot(hg_s[e], win[e], ((1,), (0,))))
    c_ig_s[...] = all_rows(parts)
    c_ig_r[img] = c_ig_s[img]
    c_ig = go(over_img(3), c_ig_s, c_ig_r, False)

    stores = []

    def store(src, dst):
        copy = pltpu.make_async_copy(src, dst, store_sem.at[len(stores)])
        copy.start()
        stores.append(copy)

    for e in range(experts):
        wog[e] = dot(act_s[e], of_expert(b_gr, e), ((0,), (0,))).astype(BF)
    store(wog, wog_hbm)

    c_out.wait_recv()
    d_out[seq] = jnp.sum(c_out_r[...].astype(F32), axis=0).astype(BF)
    e_out = go(over_seq(3), d_out, d_out, True)
    for e in range(experts):
        wig[e] = dot(hg_s[e], of_expert(b_in, e), ((0,), (0,))).astype(BF)
    store(wig, wig_hbm)
    c_ig.wait_recv()
    input_grad = jnp.sum(c_ig_r[...].astype(F32), axis=0).astype(BF)
    d_ig[seq] = input_grad
    e_ig = go(over_seq(4), d_ig, d_ig, True)
    inner = jnp.sum(slot_in * input_grad.astype(F32), axis=1, keepdims=True)
    lane = lax.broadcasted_iota(jnp.int32, (rows, 128), 1)
    d_st[seq] = jnp.where(lane == MAX_LANE, top[0], jnp.where(lane == TOTAL_LANE, total[0], inner))
    e_st = go(over_seq(5), d_st, d_st, True)

    e_out.wait_recv()
    comb_grad = dot(d_out[...].reshape(slots, depth), cot[...], ((1,), (1,)))
    across = jnp.sum(comb * comb_grad, axis=0, keepdims=True)
    comb_part = comb * (comb_grad - across)
    e_ig.wait_recv()
    every_ig = d_ig[...].reshape(slots, depth)
    disp_grad = dot(every_ig, pat[...], ((1,), (1,)))
    e_st.wait_recv()
    stats = d_st[...].reshape(slots, 128)
    scale = jnp.exp(own_max - stats[:, MAX_LANE:MAX_LANE + 1]) / stats[:, TOTAL_LANE:TOTAL_LANE + 1]
    disp = raised * scale
    logit_grad = (disp * (disp_grad - stats[:, INNER_LANE:INNER_LANE + 1]) + comb_part).astype(BF)

    e_s[...] = dot(logit_grad, pat[...], ((1,), (0,))).reshape(n_seq, rows, depth)
    e_r[seq] = e_s[seq]
    r_sum = go(over_seq(6), e_s, e_r, False)
    left = jnp.concatenate([logit_grad, disp.astype(BF)], axis=0)
    right = jnp.concatenate([router_t, every_ig], axis=0)
    pg[...] = dot(left, right, ((0,), (0,))).astype(BF)
    store(pg, pg_hbm.at[0])
    r_sum.wait_recv()
    f_buf[img] = jnp.sum(e_r[...], axis=0).astype(BF)
    r_all = go(over_img(4), f_buf, f_buf, True)
    r_all.wait_recv()
    g_buf[seq] = jnp.sum(f_buf[...].astype(F32), axis=0).astype(BF)
    r_back = go(over_seq(7), g_buf, g_buf, True)
    r_back.wait_recv()
    rg[...] = g_buf[...].astype(F32).reshape(slots, depth).T.astype(BF)
    store(rg, rg_hbm)
    for exchange in started:
        exchange.wait_send()
    for copy in stores:
        copy.wait()


def local(n_img, n_seq, patches, router, w_in, w_out, cotangent):
    _, count, depth = patches.shape
    experts, units, _ = w_in.shape
    rows = experts * SLOTS
    slots = n_seq * rows
    any_space = pl.BlockSpec(memory_space=pl.ANY)
    vmem = pltpu.VMEM
    by_seq, by_img = (n_seq, rows, depth), (n_img, rows, depth)
    return pl.pallas_call(
        functools.partial(kernel, n_img, n_seq),
        out_shape=(
            jax.ShapeDtypeStruct(patches.shape, BF),
            jax.ShapeDtypeStruct(router.shape, BF),
            jax.ShapeDtypeStruct(w_in.shape, BF),
            jax.ShapeDtypeStruct(w_out.shape, BF),
        ),
        in_specs=[any_space] * 5,
        out_specs=(any_space,) * 4,
        scratch_shapes=[
            vmem((count, depth), BF), vmem(router.shape, BF), vmem(w_in.shape, BF),
            vmem(w_out.shape, BF), vmem((count, depth), BF),
            vmem((count, depth), BF), vmem(router.shape, BF), vmem(w_in.shape, BF),
            vmem(w_out.shape, BF),
            vmem(by_seq, BF), vmem(by_seq, BF), vmem(by_seq, BF), vmem(by_seq, BF),
            vmem((n_seq, rows, 128), F32), vmem((n_seq, rows, 128), F32),
            vmem(by_img, BF), vmem(by_img, BF), vmem(by_img, BF), vmem(by_img, BF),
            vmem(by_img, BF), vmem(by_img, BF),
            vmem(by_seq, BF), vmem(by_seq, BF), vmem((n_seq, rows, 128), F32),
            vmem(by_seq, F32), vmem(by_seq, F32), vmem(by_img, BF), vmem(by_seq, BF),
            vmem((experts, n_img * SLOTS, units), BF), vmem((experts, n_img * SLOTS, units), BF),
            pltpu.SemaphoreType.DMA((5,)), pltpu.SemaphoreType.DMA((4,)),
            pltpu.SemaphoreType.DMA((8, n_seq)), pltpu.SemaphoreType.DMA((8, n_seq)),
            pltpu.SemaphoreType.DMA((5, n_img)), pltpu.SemaphoreType.DMA((5, n_img)),
        ],
        compiler_params=pltpu.CompilerParams(
            collective_id=0, has_side_effects=True, vmem_limit_bytes=48 * 1024 * 1024
        ),
    )(patches, router, w_in, w_out, cotangent)


def solution(mesh):
    placed = (
        P("img", "seq", None),
        P(),
        P("seq", "img", None),
        P("seq", "img", None),
        P("img", "seq", None),
    )
    return jax.shard_map(
        functools.partial(local, mesh.shape["img"], mesh.shape["seq"]),
        mesh=mesh,
        in_specs=placed,
        out_specs=(P("img", "seq", None), P(), P("seq", "img", None), P("seq", "img", None)),
        check_vma=False,
    )
```

```python
import functools
import math

import jax
import jax.numpy as jnp
from jax import lax
from jax.experimental import pallas as pl
from jax.experimental.pallas import tpu as pltpu
from jax.sharding import PartitionSpec as P

SLOTS = 8
MESH = pl.DeviceIdType.MESH
BF = jnp.bfloat16
F32 = jnp.float32
MAX_LANE, TOTAL_LANE, INNER_LANE = 0, 1, 2


def dot(a, b, contract):
    return lax.dot_general(a, b, (contract, ((), ())), preferred_element_type=F32)


def gelu_and_slope(values):
    coeff = math.sqrt(2.0 / math.pi)
    square = values * values
    tangent = jnp.tanh(coeff * values * (1.0 + 0.044715 * square))
    half = 0.5 * (1.0 + tangent)
    slope = half + 0.5 * values * (1.0 - tangent * tangent) * coeff * (1.0 + 3.0 * 0.044715 * square)
    return values * half, slope


class Exchange:
    def __init__(self, axis, count, send_sem, recv_sem):
        self.axis, self.count = axis, count
        self.send_sem, self.recv_sem = send_sem, recv_sem
        self.me = lax.axis_index(axis)
        self.copies = []

    def start(self, source, landing, source_is_own):
        for step in range(1, self.count):
            peer = lax.rem(self.me + step, self.count)
            copy = pltpu.make_async_remote_copy(
                src_ref=source.at[self.me if source_is_own else peer],
                dst_ref=landing.at[self.me],
                send_sem=self.send_sem.at[step],
                recv_sem=self.recv_sem.at[step],
                device_id={self.axis: peer},
                device_id_type=MESH,
            )
            copy.start()
            self.copies.append(copy)

    def wait_recv(self):
        for copy in self.copies:
            copy.wait_recv()

    def wait_send(self):
        for copy in self.copies:
            copy.wait_send()


class Copies:
    def __init__(self, send_sem, recv_sem):
        self.send_sem, self.recv_sem = send_sem, recv_sem
        self.copies = []

    def send(self, src, dst, device, at):
        copy = pltpu.make_async_remote_copy(
            src_ref=src,
            dst_ref=dst,
            send_sem=self.send_sem.at[at],
            recv_sem=self.recv_sem.at[at],
            device_id=device,
            device_id_type=MESH,
        )
        copy.start()
        self.copies.append(copy)

    def wait_recv(self):
        for copy in self.copies:
            copy.wait_recv()

    def wait_send(self):
        for copy in self.copies:
            copy.wait_send()


class Relay:
    def __init__(self, n_img, block, send_sem, recv_sem):
        img = lax.axis_index("img")
        self.chips, self.chip, self.core = n_img // 2, img // 2, lax.rem(img, 2)
        self.block, self.send_sem, self.recv_sem = block, send_sem, recv_sem
        self.copies = []

    def send(self, owner, peer, at):
        copy = pltpu.make_async_remote_copy(
            src_ref=self.block.at[owner],
            dst_ref=self.block.at[owner],
            send_sem=self.send_sem.at[at],
            recv_sem=self.recv_sem.at[at],
            device_id={"img": peer},
            device_id_type=MESH,
        )
        copy.start()
        self.copies.append(copy)

    def start(self):
        own = self.chip * 2 + self.core
        for step in range(1, self.chips):
            self.send(own, lax.rem(self.chip + step, self.chips) * 2 + self.core, step - 1)
        self.send(own, self.chip * 2 + 1 - self.core, self.chips - 1)
        return self

    def forward(self):
        for step in range(1, self.chips):
            self.copies[step - 1].wait_recv()
            owner = lax.rem(self.chip + self.chips - step, self.chips) * 2 + self.core
            self.send(owner, self.chip * 2 + 1 - self.core, self.chips - 1 + step)

    def wait_recv(self):
        for copy in self.copies[self.chips - 1:]:
            copy.wait_recv()

    def wait_send(self):
        for copy in self.copies:
            copy.wait_send()


class PairSum:
    def __init__(self, n_img, own, other, pair, landing, send_sem, recv_sem):
        img = lax.axis_index("img")
        self.chips, self.chip, self.core = n_img // 2, img // 2, lax.rem(img, 2)
        self.own, self.other, self.pair, self.landing = own, other, pair, landing
        self.send_sem, self.recv_sem = send_sem, recv_sem
        self.copies = []

    def send(self, src, dst, peer, at):
        copy = pltpu.make_async_remote_copy(
            src_ref=src,
            dst_ref=dst,
            send_sem=self.send_sem.at[at],
            recv_sem=self.recv_sem.at[at],
            device_id={"img": peer},
            device_id_type=MESH,
        )
        copy.start()
        self.copies.append(copy)

    def start(self, wide):
        for core in range(2):
            self.own[core] = wide[:, core]
        sibling = 1 - self.core
        self.send(self.own.at[sibling], self.other, self.chip * 2 + sibling, 0)
        return self

    def middle(self):
        self.copies[0].wait_recv()
        self.pair[...] = (self.own[self.core].astype(F32) + self.other[...].astype(F32)).astype(BF)
        self.landing[self.chip] = self.pair[self.chip]
        for step in range(1, self.chips):
            chip = lax.rem(self.chip + step, self.chips)
            self.send(self.pair.at[chip], self.landing.at[self.chip], chip * 2 + self.core, step)

    def result(self):
        for copy in self.copies[1:]:
            copy.wait_recv()
        return jnp.sum(self.landing[...].astype(F32), axis=0).astype(BF)

    def wait_send(self):
        for copy in self.copies:
            copy.wait_send()


def kernel(
    n_img, n_seq,
    pat_hbm, rou_hbm, win_hbm, wout_hbm, cot_hbm,
    pg_hbm, rg_hbm, wig_hbm, wog_hbm,
    pat, rou, win, wout, cot,
    pg, rg, wig, wog,
    a_in_s, a_in_r, a_gr_s, a_gr_r, a_st_s, a_st_r,
    b_in, b_gr, c_out, c_out_x, c_out_p, c_out_r, c_ig, c_ig_x, c_ig_p, c_ig_r,
    d_out, d_ig, d_st, e_s, e_r, f_buf, g_buf,
    act_s, hg_s,
    load_sem, store_sem, seq_send, seq_recv, img_send, img_recv, plane_send, plane_recv,
):
    img, seq = lax.axis_index("img"), lax.axis_index("seq")
    experts = win.shape[0]
    rows, depth = b_in.shape[1], b_in.shape[2]
    slots = n_seq * rows

    chips, chip, core = n_img // 2, img // 2, lax.rem(img, 2)

    def plane_peers():
        own = seq * 2 + core
        for step in range(1, n_seq * 2):
            peer = lax.rem(own + step, n_seq * 2)
            yield step, {"img": chip * 2 + lax.rem(peer, 2), "seq": peer // 2}, peer

    def chip_peers():
        for step in range(1, chips):
            yield step, {"img": lax.rem(chip + step, chips) * 2 + core}

    barrier = pltpu.get_barrier_semaphore()
    for _, device, _ in plane_peers():
        pl.semaphore_signal(barrier, inc=1, device_id=device, device_id_type=MESH)
    for _, device in chip_peers():
        pl.semaphore_signal(barrier, inc=1, device_id=device, device_id_type=MESH)

    loads = [
        pltpu.make_async_copy(src, dst, load_sem.at[at])
        for at, (src, dst) in enumerate(
            ((pat_hbm.at[0], pat), (rou_hbm, rou), (cot_hbm.at[0], cot), (win_hbm, win), (wout_hbm, wout))
        )
    ]
    for copy in loads[:3]:
        copy.start()

    def over_seq(at):
        return Exchange("seq", n_seq, seq_send.at[at], seq_recv.at[at])

    def relay(at, block):
        exchange = Relay(n_img, block, img_send.at[at], img_recv.at[at])
        started.append(exchange)
        return exchange.start()

    def pair_sum(at, wide, *buffers):
        exchange = PairSum(n_img, *buffers, img_send.at[at], img_recv.at[at])
        started.append(exchange)
        return exchange.start(wide)

    started = []

    def go(exchange, source, landing, own):
        exchange.start(source, landing, own)
        started.append(exchange)
        return exchange

    loads[1].wait()
    router_t = rou[...]
    loads[0].wait()
    logits = dot(router_t, pat[...], ((1,), (1,)))
    own_max = jnp.max(logits, axis=1, keepdims=True)
    raised = jnp.exp(logits - own_max)
    own_total = jnp.sum(raised, axis=1, keepdims=True)
    part_in = dot((raised * (1.0 / own_total)).astype(BF), pat[...], ((1,), (0,)))
    lane = lax.broadcasted_iota(jnp.int32, (slots, 128), 1)
    a_st_s[...] = jnp.where(lane == MAX_LANE, own_max, own_total).reshape(n_seq, rows, 128)
    a_in_s[...] = part_in.astype(BF).reshape(n_seq, rows, depth)
    a_st_r[seq] = a_st_s[seq]
    a_in_r[seq] = a_in_s[seq]
    pl.semaphore_wait(barrier, n_seq * 2 - 1 + chips - 1)
    a_st = go(over_seq(0), a_st_s, a_st_r, False)
    a_in = go(over_seq(1), a_in_s, a_in_r, False)
    for copy in loads[3:]:
        copy.start()

    comb = jnp.exp(logits - jnp.max(logits, axis=0, keepdims=True))
    comb = comb * (1.0 / jnp.sum(comb, axis=0, keepdims=True))
    loads[2].wait()
    part_gr = dot(comb.astype(BF), cot[...], ((1,), (0,)))
    a_gr_s[...] = part_gr.astype(BF).reshape(n_seq, rows, depth)
    a_gr_r[seq] = a_gr_s[seq]
    a_gr = go(over_seq(2), a_gr_s, a_gr_r, False)

    a_st.wait_recv()
    a_in.wait_recv()
    stats = a_st_r[...]
    maxes, totals = stats[:, :, MAX_LANE:MAX_LANE + 1], stats[:, :, TOTAL_LANE:TOTAL_LANE + 1]
    top = jnp.max(maxes, axis=0, keepdims=True)
    shares = totals * jnp.exp(maxes - top)
    total = jnp.sum(shares, axis=0, keepdims=True)
    slot_in = jnp.sum(a_in_r[...].astype(F32) * (shares / total), axis=0)
    b_in[img] = slot_in.astype(BF)
    g_in = relay(0, b_in)
    a_gr.wait_recv()
    b_gr[img] = jnp.sum(a_gr_r[...].astype(F32), axis=0).astype(BF)
    g_gr = relay(1, b_gr)

    def of_expert(buffer, e):
        wide = buffer[...].astype(F32).reshape(n_img, experts, SLOTS, depth)
        return wide[:, e].reshape(n_img * SLOTS, depth).astype(BF)

    def all_rows(parts):
        wide = [part.reshape(n_img, 1, SLOTS, depth) for part in parts]
        wide = jnp.concatenate(wide, axis=1).reshape(n_img // 2, 2, rows, depth)
        return wide.astype(BF)

    loads[3].wait()
    g_in.forward()
    g_in.wait_recv()
    slopes, parts = [], []
    loads[4].wait()
    for e in range(experts):
        hidden = dot(of_expert(b_in, e), win[e], ((1,), (1,)))
        active, slope = gelu_and_slope(hidden)
        slopes.append(slope)
        act_s[e] = active.astype(BF)
        parts.append(dot(act_s[e], wout[e], ((1,), (0,))))
    out_sum = pair_sum(2, all_rows(parts), c_out, c_out_x, c_out_p, c_out_r)
    g_gr.forward()
    g_gr.wait_recv()
    parts = []
    for e in range(experts):
        act_grad = dot(of_expert(b_gr, e), wout[e], ((1,), (1,)))
        hg_s[e] = (act_grad * slopes[e]).astype(BF)
        parts.append(dot(hg_s[e], win[e], ((1,), (0,))))
    ig_sum = pair_sum(3, all_rows(parts), c_ig, c_ig_x, c_ig_p, c_ig_r)
    out_sum.middle()
    ig_sum.middle()

    stores = []

    def store(src, dst):
        copy = pltpu.make_async_copy(src, dst, store_sem.at[len(stores)])
        copy.start()
        stores.append(copy)

    for e in range(experts):
        wog[e] = dot(act_s[e], of_expert(b_gr, e), ((0,), (0,))).astype(BF)
    store(wog, wog_hbm)

    d_out[seq] = out_sum.result()
    e_out = go(over_seq(3), d_out, d_out, True)
    for e in range(experts):
        wig[e] = dot(hg_s[e], of_expert(b_in, e), ((0,), (0,))).astype(BF)
    store(wig, wig_hbm)
    input_grad = ig_sum.result()
    d_ig[seq] = input_grad
    e_ig = go(over_seq(4), d_ig, d_ig, True)
    inner = jnp.sum(slot_in * input_grad.astype(F32), axis=1, keepdims=True)
    lane = lax.broadcasted_iota(jnp.int32, (rows, 128), 1)
    d_st[seq] = jnp.where(lane == MAX_LANE, top[0], jnp.where(lane == TOTAL_LANE, total[0], inner))
    e_st = go(over_seq(5), d_st, d_st, True)

    e_out.wait_recv()
    comb_grad = dot(d_out[...].reshape(slots, depth), cot[...], ((1,), (1,)))
    across = jnp.sum(comb * comb_grad, axis=0, keepdims=True)
    comb_part = comb * (comb_grad - across)
    e_ig.wait_recv()
    every_ig = d_ig[...].reshape(slots, depth)
    disp_grad = dot(every_ig, pat[...], ((1,), (1,)))
    e_st.wait_recv()
    stats = d_st[...].reshape(slots, 128)
    scale = jnp.exp(own_max - stats[:, MAX_LANE:MAX_LANE + 1]) / stats[:, TOTAL_LANE:TOTAL_LANE + 1]
    disp = raised * scale
    logit_grad = (disp * (disp_grad - stats[:, INNER_LANE:INNER_LANE + 1]) + comb_part).astype(BF)

    router_part = dot(logit_grad, pat[...], ((1,), (0,))).reshape(n_seq, rows, depth)
    half = depth // 2
    for side in range(2):
        e_s[:, side] = router_part[:, :, side * half:(side + 1) * half]
    e_r[seq * 2 + core] = e_s[seq, core]

    def to_plane(at, source, landing):
        copies = Copies(plane_send.at[at], plane_recv.at[at])
        for step, device, peer in plane_peers():
            copies.send(source(peer), landing, device, step)
        started.append(copies)
        return copies

    r_sum = to_plane(0, lambda peer: e_s.at[peer // 2, lax.rem(peer, 2)], e_r.at[seq * 2 + core])
    left = jnp.concatenate([logit_grad, disp.astype(BF)], axis=0)
    right = jnp.concatenate([router_t, every_ig], axis=0)
    pg[...] = dot(left, right, ((0,), (0,))).astype(BF)
    store(pg, pg_hbm.at[0])
    r_sum.wait_recv()
    f_buf[chip] = jnp.sum(e_r[...], axis=0)
    r_all = Copies(img_send.at[4], img_recv.at[4])
    for step, device in chip_peers():
        r_all.send(f_buf.at[chip], f_buf.at[chip], device, step)
    started.append(r_all)
    r_all.wait_recv()
    own_block = g_buf.at[seq * 2 + core]
    own_block[...] = jnp.sum(f_buf[...], axis=0).astype(BF)
    to_plane(1, lambda peer: own_block, own_block).wait_recv()
    for at in range(n_seq):
        rg[at] = jnp.concatenate([g_buf[2 * at], g_buf[2 * at + 1]], axis=1)
    store(rg, rg_hbm)
    for exchange in started:
        exchange.wait_send()
    for copy in stores:
        copy.wait()


def local(n_img, n_seq, patches, router, w_in, w_out, cotangent):
    _, count, depth = patches.shape
    experts, units, _ = w_in.shape
    rows = experts * SLOTS
    slots = n_seq * rows
    any_space = pl.BlockSpec(memory_space=pl.ANY)
    vmem = pltpu.VMEM
    by_seq, by_img = (n_seq, rows, depth), (n_img, rows, depth)
    by_chip, half = (n_img // 2, rows, depth), (rows, depth // 2)
    patch_grad, router_grad, w_in_grad, w_out_grad = pl.pallas_call(
        functools.partial(kernel, n_img, n_seq),
        out_shape=(
            jax.ShapeDtypeStruct(patches.shape, BF),
            jax.ShapeDtypeStruct(by_seq, BF),
            jax.ShapeDtypeStruct(w_in.shape, BF),
            jax.ShapeDtypeStruct(w_out.shape, BF),
        ),
        in_specs=[pl.BlockSpec(memory_space=pltpu.HBM)] * 5,
        out_specs=(any_space,) * 4,
        scratch_shapes=[
            vmem((count, depth), BF), vmem((slots, depth), BF), vmem(w_in.shape, BF),
            vmem(w_out.shape, BF), vmem((count, depth), BF),
            vmem((count, depth), BF), vmem(by_seq, BF), vmem(w_in.shape, BF), vmem(w_out.shape, BF),
            vmem(by_seq, BF), vmem(by_seq, BF), vmem(by_seq, BF), vmem(by_seq, BF),
            vmem((n_seq, rows, 128), F32), vmem((n_seq, rows, 128), F32),
            vmem(by_img, BF), vmem(by_img, BF),
            vmem((2,) + by_chip, BF), vmem(by_chip, BF), vmem(by_chip, BF), vmem(by_chip, BF),
            vmem((2,) + by_chip, BF), vmem(by_chip, BF), vmem(by_chip, BF), vmem(by_chip, BF),
            vmem(by_seq, BF), vmem(by_seq, BF), vmem((n_seq, rows, 128), F32),
            vmem((n_seq, 2) + half, F32), vmem((n_seq * 2,) + half, F32),
            vmem((n_img // 2,) + half, F32), vmem((n_seq * 2,) + half, BF),
            vmem((experts, n_img * SLOTS, units), BF), vmem((experts, n_img * SLOTS, units), BF),
            pltpu.SemaphoreType.DMA((5,)), pltpu.SemaphoreType.DMA((4,)),
            pltpu.SemaphoreType.DMA((8, n_seq)), pltpu.SemaphoreType.DMA((8, n_seq)),
            pltpu.SemaphoreType.DMA((5, n_img)), pltpu.SemaphoreType.DMA((5, n_img)),
            pltpu.SemaphoreType.DMA((2, 2 * n_seq)), pltpu.SemaphoreType.DMA((2, 2 * n_seq)),
        ],
        compiler_params=pltpu.CompilerParams(
            collective_id=0, has_side_effects=True, vmem_limit_bytes=60 * 1024 * 1024
        ),
    )(patches, router.T, w_in, w_out, cotangent)
    return patch_grad, router_grad.reshape(slots, depth).T, w_in_grad, w_out_grad


def solution(mesh):
    placed = (
        P("img", "seq", None),
        P(),
        P("seq", "img", None),
        P("seq", "img", None),
        P("img", "seq", None),
    )
    return jax.shard_map(
        functools.partial(local, mesh.shape["img"], mesh.shape["seq"]),
        mesh=mesh,
        in_specs=placed,
        out_specs=(P("img", "seq", None), P(), P("seq", "img", None), P("seq", "img", None)),
        check_vma=False,
    )
```

```python
import functools
import math

import jax
import jax.numpy as jnp
from jax import lax
from jax.experimental import pallas as pl
from jax.experimental.pallas import tpu as pltpu
from jax.sharding import PartitionSpec as P

SLOTS = 8
MESH = pl.DeviceIdType.MESH
BF = jnp.bfloat16
F32 = jnp.float32
CHUNK = 256
MAX_LANE, TOTAL_LANE, INNER_LANE = 0, 1, 2


def dot(a, b, contract):
    return lax.dot_general(a, b, (contract, ((), ())), preferred_element_type=F32)


def gelu_and_slope(values):
    coeff = math.sqrt(2.0 / math.pi)
    square = values * values
    tangent = jnp.tanh(coeff * values * (1.0 + 0.044715 * square))
    half = 0.5 * (1.0 + tangent)
    slope = half + 0.5 * values * (1.0 - tangent * tangent) * coeff * (1.0 + 3.0 * 0.044715 * square)
    return values * half, slope


class Exchange:
    def __init__(self, axis, count, send_sem, recv_sem):
        self.axis, self.count = axis, count
        self.send_sem, self.recv_sem = send_sem, recv_sem
        self.me = lax.axis_index(axis)
        self.copies = []

    def start(self, source, landing, source_is_own):
        for step in range(1, self.count):
            peer = lax.rem(self.me + step, self.count)
            copy = pltpu.make_async_remote_copy(
                src_ref=source.at[self.me if source_is_own else peer],
                dst_ref=landing.at[self.me],
                send_sem=self.send_sem.at[step],
                recv_sem=self.recv_sem.at[step],
                device_id={self.axis: peer},
                device_id_type=MESH,
            )
            copy.start()
            self.copies.append(copy)

    def wait_recv(self):
        for copy in self.copies:
            copy.wait_recv()

    def wait_send(self):
        for copy in self.copies:
            copy.wait_send()


def of_expert(buffer, e, experts):
    n_img, rows, depth = buffer.shape
    wide = buffer[...].astype(F32).reshape(n_img, experts, SLOTS, depth)
    return wide[:, e].reshape(n_img * SLOTS, depth).astype(BF)


class Copies:
    def __init__(self, send_sem, recv_sem):
        self.send_sem, self.recv_sem = send_sem, recv_sem
        self.copies = []

    def send(self, src, dst, device, at):
        copy = pltpu.make_async_remote_copy(
            src_ref=src,
            dst_ref=dst,
            send_sem=self.send_sem.at[at],
            recv_sem=self.recv_sem.at[at],
            device_id=device,
            device_id_type=MESH,
        )
        copy.start()
        self.copies.append(copy)

    def wait_recv(self):
        for copy in self.copies:
            copy.wait_recv()

    def wait_send(self):
        for copy in self.copies:
            copy.wait_send()


class Relay:
    def __init__(self, n_img, block, send_sem, recv_sem):
        img = lax.axis_index("img")
        self.chips, self.chip, self.core = n_img // 2, img // 2, lax.rem(img, 2)
        self.block, self.send_sem, self.recv_sem = block, send_sem, recv_sem
        self.copies = []

    def send(self, owner, peer, at):
        copy = pltpu.make_async_remote_copy(
            src_ref=self.block.at[owner],
            dst_ref=self.block.at[owner],
            send_sem=self.send_sem.at[at],
            recv_sem=self.recv_sem.at[at],
            device_id={"img": peer},
            device_id_type=MESH,
        )
        copy.start()
        self.copies.append(copy)

    def start(self):
        own = self.chip * 2 + self.core
        for step in range(1, self.chips):
            self.send(own, lax.rem(self.chip + step, self.chips) * 2 + self.core, step - 1)
        self.send(own, self.chip * 2 + 1 - self.core, self.chips - 1)
        return self

    def forward(self):
        for step in range(1, self.chips):
            self.copies[step - 1].wait_recv()
            owner = lax.rem(self.chip + self.chips - step, self.chips) * 2 + self.core
            self.send(owner, self.chip * 2 + 1 - self.core, self.chips - 1 + step)

    def wait_recv(self):
        for copy in self.copies[self.chips - 1:]:
            copy.wait_recv()

    def wait_send(self):
        for copy in self.copies:
            copy.wait_send()


class PairSum:
    def __init__(self, n_img, own, other, pair, landing, send_sem, recv_sem):
        img = lax.axis_index("img")
        self.chips, self.chip, self.core = n_img // 2, img // 2, lax.rem(img, 2)
        self.own, self.other, self.pair, self.landing = own, other, pair, landing
        self.send_sem, self.recv_sem = send_sem, recv_sem
        self.copies = []

    def send(self, src, dst, peer, at):
        copy = pltpu.make_async_remote_copy(
            src_ref=src,
            dst_ref=dst,
            send_sem=self.send_sem.at[at],
            recv_sem=self.recv_sem.at[at],
            device_id={"img": peer},
            device_id_type=MESH,
        )
        copy.start()
        self.copies.append(copy)

    def start(self, wide):
        for core in range(2):
            self.own[core] = wide[:, core]
        sibling = 1 - self.core
        self.send(self.own.at[sibling], self.other, self.chip * 2 + sibling, 0)
        return self

    def middle(self):
        self.copies[0].wait_recv()
        self.pair[...] = (self.own[self.core].astype(F32) + self.other[...].astype(F32)).astype(BF)
        self.landing[self.chip] = self.pair[self.chip]
        for step in range(1, self.chips):
            chip = lax.rem(self.chip + step, self.chips)
            self.send(self.pair.at[chip], self.landing.at[self.chip], chip * 2 + self.core, step)

    def result(self):
        for copy in self.copies[1:]:
            copy.wait_recv()
        return jnp.sum(self.landing[...].astype(F32), axis=0).astype(BF)

    def wait_send(self):
        for copy in self.copies:
            copy.wait_send()


def kernel(
    n_img, n_seq,
    pat_hbm, rou_hbm, win_hbm, wout_hbm, cot_hbm,
    left_hbm, right_hbm, rg_hbm, act_hbm, hg_hbm, in_hbm, gr_hbm,
    pat, rou, win, wout, cot,
    left, right, rg,
    a_in_s, a_in_r, a_gr_s, a_gr_r, a_st_s, a_st_r,
    b_in, b_gr, c_out, c_out_x, c_out_p, c_out_r, c_ig, c_ig_x, c_ig_p, c_ig_r,
    d_out, d_ig, d_st, e_s, e_r, f_buf, g_buf,
    act_s, hg_s,
    load_sem, store_sem, seq_send, seq_recv, img_send, img_recv, plane_send, plane_recv,
):
    img, seq = lax.axis_index("img"), lax.axis_index("seq")
    experts = win.shape[0]
    rows, depth = b_in.shape[1], b_in.shape[2]
    slots = n_seq * rows

    chips, chip, core = n_img // 2, img // 2, lax.rem(img, 2)

    def plane_peers():
        own = seq * 2 + core
        for step in range(1, n_seq * 2):
            peer = lax.rem(own + step, n_seq * 2)
            yield step, {"img": chip * 2 + lax.rem(peer, 2), "seq": peer // 2}, peer

    def chip_peers():
        for step in range(1, chips):
            yield step, {"img": lax.rem(chip + step, chips) * 2 + core}

    barrier = pltpu.get_barrier_semaphore()
    for _, device, _ in plane_peers():
        pl.semaphore_signal(barrier, inc=1, device_id=device, device_id_type=MESH)
    for _, device in chip_peers():
        pl.semaphore_signal(barrier, inc=1, device_id=device, device_id_type=MESH)

    loads = [
        pltpu.make_async_copy(src, dst, load_sem.at[at])
        for at, (src, dst) in enumerate(
            ((pat_hbm.at[0], pat), (rou_hbm, rou), (cot_hbm.at[0], cot), (win_hbm, win), (wout_hbm, wout))
        )
    ]
    for copy in loads[:3]:
        copy.start()

    def over_seq(at):
        return Exchange("seq", n_seq, seq_send.at[at], seq_recv.at[at])

    def relay(at, block):
        exchange = Relay(n_img, block, img_send.at[at], img_recv.at[at])
        started.append(exchange)
        return exchange.start()

    def pair_sum(at, wide, *buffers):
        exchange = PairSum(n_img, *buffers, img_send.at[at], img_recv.at[at])
        started.append(exchange)
        return exchange.start(wide)

    started = []

    def go(exchange, source, landing, own):
        exchange.start(source, landing, own)
        started.append(exchange)
        return exchange

    loads[1].wait()
    router_t = rou[...]
    loads[0].wait()
    logits = dot(router_t, pat[...], ((1,), (1,)))
    own_max = jnp.max(logits, axis=1, keepdims=True)
    raised = jnp.exp(logits - own_max)
    own_total = jnp.sum(raised, axis=1, keepdims=True)
    part_in = dot((raised * (1.0 / own_total)).astype(BF), pat[...], ((1,), (0,)))
    lane = lax.broadcasted_iota(jnp.int32, (slots, 128), 1)
    a_st_s[...] = jnp.where(lane == MAX_LANE, own_max, own_total).reshape(n_seq, rows, 128)
    a_in_s[...] = part_in.astype(BF).reshape(n_seq, rows, depth)
    a_st_r[seq] = a_st_s[seq]
    a_in_r[seq] = a_in_s[seq]
    pl.semaphore_wait(barrier, n_seq * 2 - 1 + chips - 1)
    a_st = go(over_seq(0), a_st_s, a_st_r, False)
    a_in = go(over_seq(1), a_in_s, a_in_r, False)
    for copy in loads[3:]:
        copy.start()

    comb = jnp.exp(logits - jnp.max(logits, axis=0, keepdims=True))
    comb = comb * (1.0 / jnp.sum(comb, axis=0, keepdims=True))
    loads[2].wait()
    part_gr = dot(comb.astype(BF), cot[...], ((1,), (0,)))
    a_gr_s[...] = part_gr.astype(BF).reshape(n_seq, rows, depth)
    a_gr_r[seq] = a_gr_s[seq]
    a_gr = go(over_seq(2), a_gr_s, a_gr_r, False)

    a_st.wait_recv()
    a_in.wait_recv()
    stats = a_st_r[...]
    maxes, totals = stats[:, :, MAX_LANE:MAX_LANE + 1], stats[:, :, TOTAL_LANE:TOTAL_LANE + 1]
    top = jnp.max(maxes, axis=0, keepdims=True)
    shares = totals * jnp.exp(maxes - top)
    total = jnp.sum(shares, axis=0, keepdims=True)
    slot_in = jnp.sum(a_in_r[...].astype(F32) * (shares / total), axis=0)
    b_in[img] = slot_in.astype(BF)
    g_in = relay(0, b_in)
    a_gr.wait_recv()
    b_gr[img] = jnp.sum(a_gr_r[...].astype(F32), axis=0).astype(BF)
    g_gr = relay(1, b_gr)

    def all_rows(parts):
        wide = [part.reshape(n_img, 1, SLOTS, depth) for part in parts]
        wide = jnp.concatenate(wide, axis=1).reshape(n_img // 2, 2, rows, depth)
        return wide.astype(BF)

    loads[3].wait()
    g_in.forward()
    g_in.wait_recv()
    slopes, parts = [], []
    loads[4].wait()
    for e in range(experts):
        hidden = dot(of_expert(b_in, e, experts), win[e], ((1,), (1,)))
        active, slope = gelu_and_slope(hidden)
        slopes.append(slope)
        act_s[e] = active.astype(BF)
        parts.append(dot(act_s[e], wout[e], ((1,), (0,))))
    out_sum = pair_sum(2, all_rows(parts), c_out, c_out_x, c_out_p, c_out_r)
    g_gr.forward()
    g_gr.wait_recv()
    parts = []
    for e in range(experts):
        act_grad = dot(of_expert(b_gr, e, experts), wout[e], ((1,), (1,)))
        hg_s[e] = (act_grad * slopes[e]).astype(BF)
        parts.append(dot(hg_s[e], win[e], ((1,), (0,))))
    ig_sum = pair_sum(3, all_rows(parts), c_ig, c_ig_x, c_ig_p, c_ig_r)
    out_sum.middle()
    ig_sum.middle()

    stores = []

    def store(src, dst):
        copy = pltpu.make_async_copy(src, dst, store_sem.at[len(stores)])
        copy.start()
        stores.append(copy)

    store(act_s, act_hbm)
    store(hg_s, hg_hbm)
    store(b_in, in_hbm)
    store(b_gr, gr_hbm)

    d_out[seq] = out_sum.result()
    e_out = go(over_seq(3), d_out, d_out, True)
    input_grad = ig_sum.result()
    d_ig[seq] = input_grad
    e_ig = go(over_seq(4), d_ig, d_ig, True)
    inner = jnp.sum(slot_in * input_grad.astype(F32), axis=1, keepdims=True)
    lane = lax.broadcasted_iota(jnp.int32, (rows, 128), 1)
    d_st[seq] = jnp.where(lane == MAX_LANE, top[0], jnp.where(lane == TOTAL_LANE, total[0], inner))
    e_st = go(over_seq(5), d_st, d_st, True)

    e_out.wait_recv()
    comb_grad = dot(d_out[...].reshape(slots, depth), cot[...], ((1,), (1,)))
    across = jnp.sum(comb * comb_grad, axis=0, keepdims=True)
    comb_part = comb * (comb_grad - across)
    e_ig.wait_recv()
    every_ig = d_ig[...].reshape(slots, depth)
    disp_grad = dot(every_ig, pat[...], ((1,), (1,)))
    e_st.wait_recv()
    stats = d_st[...].reshape(slots, 128)
    scale = jnp.exp(own_max - stats[:, MAX_LANE:MAX_LANE + 1]) / stats[:, TOTAL_LANE:TOTAL_LANE + 1]
    disp = raised * scale
    logit_grad = (disp * (disp_grad - stats[:, INNER_LANE:INNER_LANE + 1]) + comb_part).astype(BF)

    router_part = dot(logit_grad, pat[...], ((1,), (0,))).reshape(n_seq, rows, depth)
    half = depth // 2
    for side in range(2):
        e_s[:, side] = router_part[:, :, side * half:(side + 1) * half]
    e_r[seq * 2 + core] = e_s[seq, core]

    def to_plane(at, source, landing):
        copies = Copies(plane_send.at[at], plane_recv.at[at])
        for step, device, peer in plane_peers():
            copies.send(source(peer), landing, device, step)
        started.append(copies)
        return copies

    r_sum = to_plane(0, lambda peer: e_s.at[peer // 2, lax.rem(peer, 2)], e_r.at[seq * 2 + core])
    left[:slots] = logit_grad
    left[slots:] = disp.astype(BF)
    right[:slots] = router_t
    right[slots:] = every_ig
    store(left, left_hbm)
    store(right, right_hbm)
    r_sum.wait_recv()
    f_buf[chip] = jnp.sum(e_r[...], axis=0)
    r_all = Copies(img_send.at[4], img_recv.at[4])
    for step, device in chip_peers():
        r_all.send(f_buf.at[chip], f_buf.at[chip], device, step)
    started.append(r_all)
    r_all.wait_recv()
    own_block = g_buf.at[seq * 2 + core]
    own_block[...] = jnp.sum(f_buf[...], axis=0).astype(BF)
    to_plane(1, lambda peer: own_block, own_block).wait_recv()
    for at in range(n_seq):
        rg[at] = jnp.concatenate([g_buf[2 * at], g_buf[2 * at + 1]], axis=1)
    store(rg, rg_hbm)
    for exchange in started:
        exchange.wait_send()
    for copy in stores:
        copy.wait()


def write_kernel(
    left_hbm, right_hbm, rg_hbm, act_hbm, hg_hbm, in_hbm, gr_hbm,
    pg_out, rg_out, wig_out, wog_out,
    left, right, rg_in, act, hg, b_in, b_gr,
    pg, rg, wig, wog,
    load_sem, store_sem,
):
    experts, count = act.shape[0], left.shape[1]
    sources = (left_hbm, right_hbm, act_hbm, gr_hbm, hg_hbm, in_hbm, rg_hbm)
    loads = [
        pltpu.make_async_copy(src, dst, load_sem.at[at])
        for at, (src, dst) in enumerate(zip(sources, (left, right, act, b_gr, hg, b_in, rg_in)))
    ]
    for copy in loads:
        copy.start()
    stores = []

    def store(src, dst):
        copy = pltpu.make_async_copy(src, dst, store_sem.at[len(stores)])
        copy.start()
        stores.append(copy)

    loads[0].wait()
    loads[1].wait()
    for at in range(0, count, CHUNK):
        span = pl.ds(at, CHUNK)
        pg[span] = dot(left[:, span], right[...], ((0,), (0,))).astype(BF)
        store(pg.at[span], pg_out.at[0, span])
    loads[2].wait()
    loads[3].wait()
    for e in range(experts):
        wog[e] = dot(act[e], of_expert(b_gr, e, experts), ((0,), (0,))).astype(BF)
        store(wog.at[e], wog_out.at[e])
    loads[4].wait()
    loads[5].wait()
    for e in range(experts):
        wig[e] = dot(hg[e], of_expert(b_in, e, experts), ((0,), (0,))).astype(BF)
        store(wig.at[e], wig_out.at[e])
    loads[6].wait()
    rg[...] = rg_in[...].reshape(rg.shape)
    store(rg, rg_out)
    for copy in stores:
        copy.wait()


def local(n_img, n_seq, patches, router, w_in, w_out, cotangent):
    _, count, depth = patches.shape
    experts, units, _ = w_in.shape
    rows = experts * SLOTS
    slots = n_seq * rows
    by_unit = (experts, n_img * SLOTS, units)
    any_space = pl.BlockSpec(memory_space=pltpu.HBM)
    vmem = pltpu.VMEM
    by_seq, by_img = (n_seq, rows, depth), (n_img, rows, depth)
    by_chip, half = (n_img // 2, rows, depth), (rows, depth // 2)
    parts = pl.pallas_call(
        functools.partial(kernel, n_img, n_seq),
        out_shape=(
            jax.ShapeDtypeStruct((2 * slots, count), BF),
            jax.ShapeDtypeStruct((2 * slots, depth), BF),
            jax.ShapeDtypeStruct(by_seq, BF),
            jax.ShapeDtypeStruct(by_unit, BF),
            jax.ShapeDtypeStruct(by_unit, BF),
            jax.ShapeDtypeStruct(by_img, BF),
            jax.ShapeDtypeStruct(by_img, BF),
        ),
        in_specs=[any_space] * 5,
        out_specs=(any_space,) * 7,
        scratch_shapes=[
            vmem((count, depth), BF), vmem((slots, depth), BF), vmem(w_in.shape, BF),
            vmem(w_out.shape, BF), vmem((count, depth), BF),
            vmem((2 * slots, count), BF), vmem((2 * slots, depth), BF), vmem(by_seq, BF),
            vmem(by_seq, BF), vmem(by_seq, BF), vmem(by_seq, BF), vmem(by_seq, BF),
            vmem((n_seq, rows, 128), F32), vmem((n_seq, rows, 128), F32),
            vmem(by_img, BF), vmem(by_img, BF),
            vmem((2,) + by_chip, BF), vmem(by_chip, BF), vmem(by_chip, BF), vmem(by_chip, BF),
            vmem((2,) + by_chip, BF), vmem(by_chip, BF), vmem(by_chip, BF), vmem(by_chip, BF),
            vmem(by_seq, BF), vmem(by_seq, BF), vmem((n_seq, rows, 128), F32),
            vmem((n_seq, 2) + half, F32), vmem((n_seq * 2,) + half, F32),
            vmem((n_img // 2,) + half, F32), vmem((n_seq * 2,) + half, BF),
            vmem(by_unit, BF), vmem(by_unit, BF),
            pltpu.SemaphoreType.DMA((5,)), pltpu.SemaphoreType.DMA((7,)),
            pltpu.SemaphoreType.DMA((8, n_seq)), pltpu.SemaphoreType.DMA((8, n_seq)),
            pltpu.SemaphoreType.DMA((5, n_img)), pltpu.SemaphoreType.DMA((5, n_img)),
            pltpu.SemaphoreType.DMA((2, 2 * n_seq)), pltpu.SemaphoreType.DMA((2, 2 * n_seq)),
        ],
        compiler_params=pltpu.CompilerParams(
            collective_id=0, has_side_effects=True, vmem_limit_bytes=60 * 1024 * 1024
        ),
    )(patches, router.T, w_in, w_out, cotangent)
    patch_grad, router_grad, w_in_grad, w_out_grad = pl.pallas_call(
        write_kernel,
        out_shape=(
            jax.ShapeDtypeStruct(patches.shape, BF),
            jax.ShapeDtypeStruct((slots, depth), BF),
            jax.ShapeDtypeStruct(w_in.shape, BF),
            jax.ShapeDtypeStruct(w_out.shape, BF),
        ),
        in_specs=[any_space] * 7,
        out_specs=(any_space,) * 4,
        scratch_shapes=[
            vmem((2 * slots, count), BF), vmem((2 * slots, depth), BF), vmem(by_seq, BF),
            vmem(by_unit, BF), vmem(by_unit, BF), vmem(by_img, BF), vmem(by_img, BF),
            vmem((count, depth), BF), vmem((slots, depth), BF), vmem(w_in.shape, BF), vmem(w_out.shape, BF),
            pltpu.SemaphoreType.DMA((7,)), pltpu.SemaphoreType.DMA((3 + 2 * experts + count // CHUNK,)),
        ],
        compiler_params=pltpu.CompilerParams(vmem_limit_bytes=60 * 1024 * 1024),
    )(*parts)
    return patch_grad, router_grad.T, w_in_grad, w_out_grad


def solution(mesh):
    placed = (
        P("img", "seq", None),
        P(),
        P("seq", "img", None),
        P("seq", "img", None),
        P("img", "seq", None),
    )
    return jax.shard_map(
        functools.partial(local, mesh.shape["img"], mesh.shape["seq"]),
        mesh=mesh,
        in_specs=placed,
        out_specs=(P("img", "seq", None), P(), P("seq", "img", None), P("seq", "img", None)),
        check_vma=False,
    )
```

```python
import functools
import math

import jax
import jax.numpy as jnp
from jax import lax
from jax.experimental import pallas as pl
from jax.experimental.pallas import tpu as pltpu
from jax.sharding import PartitionSpec as P

SLOTS = 8
MESH = pl.DeviceIdType.MESH
BF = jnp.bfloat16
F32 = jnp.float32
CHUNK = 256
MAX_LANE, TOTAL_LANE, INNER_LANE = 0, 1, 2


def dot(a, b, contract):
    return lax.dot_general(a, b, (contract, ((), ())), preferred_element_type=F32)


def gelu_and_slope(values):
    coeff = math.sqrt(2.0 / math.pi)
    square = values * values
    tangent = jnp.tanh(coeff * values * (1.0 + 0.044715 * square))
    half = 0.5 * (1.0 + tangent)
    slope = half + 0.5 * values * (1.0 - tangent * tangent) * coeff * (1.0 + 3.0 * 0.044715 * square)
    return values * half, slope


class Exchange:
    def __init__(self, axis, count, send_sem, recv_sem):
        self.axis, self.count = axis, count
        self.send_sem, self.recv_sem = send_sem, recv_sem
        self.me = lax.axis_index(axis)
        self.copies = []

    def start(self, source, landing, source_is_own):
        for step in range(1, self.count):
            peer = lax.rem(self.me + step, self.count)
            copy = pltpu.make_async_remote_copy(
                src_ref=source.at[self.me if source_is_own else peer],
                dst_ref=landing.at[self.me],
                send_sem=self.send_sem.at[step],
                recv_sem=self.recv_sem.at[step],
                device_id={self.axis: peer},
                device_id_type=MESH,
            )
            copy.start()
            self.copies.append(copy)

    def wait_recv(self):
        for copy in self.copies:
            copy.wait_recv()

    def wait_send(self):
        for copy in self.copies:
            copy.wait_send()


def of_expert(buffer, e, experts):
    n_img, rows, depth = buffer.shape
    wide = buffer[...].astype(F32).reshape(n_img, experts, SLOTS, depth)
    return wide[:, e].reshape(n_img * SLOTS, depth).astype(BF)


class Copies:
    def __init__(self, send_sem, recv_sem):
        self.send_sem, self.recv_sem = send_sem, recv_sem
        self.copies = []

    def send(self, src, dst, device, at):
        copy = pltpu.make_async_remote_copy(
            src_ref=src,
            dst_ref=dst,
            send_sem=self.send_sem.at[at],
            recv_sem=self.recv_sem.at[at],
            device_id=device,
            device_id_type=MESH,
        )
        copy.start()
        self.copies.append(copy)

    def wait_recv(self):
        for copy in self.copies:
            copy.wait_recv()

    def wait_send(self):
        for copy in self.copies:
            copy.wait_send()


class Relay:
    def __init__(self, n_img, block, send_sem, recv_sem):
        img = lax.axis_index("img")
        self.chips, self.chip, self.core = n_img // 2, img // 2, lax.rem(img, 2)
        self.block, self.send_sem, self.recv_sem = block, send_sem, recv_sem
        self.copies = []

    def send(self, owner, peer, at):
        copy = pltpu.make_async_remote_copy(
            src_ref=self.block.at[owner],
            dst_ref=self.block.at[owner],
            send_sem=self.send_sem.at[at],
            recv_sem=self.recv_sem.at[at],
            device_id={"img": peer},
            device_id_type=MESH,
        )
        copy.start()
        self.copies.append(copy)

    def start(self):
        own = self.chip * 2 + self.core
        for step in range(1, self.chips):
            self.send(own, lax.rem(self.chip + step, self.chips) * 2 + self.core, step - 1)
        self.send(own, self.chip * 2 + 1 - self.core, self.chips - 1)
        return self

    def forward(self):
        for step in range(1, self.chips):
            self.copies[step - 1].wait_recv()
            owner = lax.rem(self.chip + self.chips - step, self.chips) * 2 + self.core
            self.send(owner, self.chip * 2 + 1 - self.core, self.chips - 1 + step)

    def wait_recv(self):
        for copy in self.copies[self.chips - 1:]:
            copy.wait_recv()

    def wait_send(self):
        for copy in self.copies:
            copy.wait_send()


class PairSum:
    def __init__(self, n_img, own, other, pair, landing, send_sem, recv_sem):
        img = lax.axis_index("img")
        self.chips, self.chip, self.core = n_img // 2, img // 2, lax.rem(img, 2)
        self.own, self.other, self.pair, self.landing = own, other, pair, landing
        self.send_sem, self.recv_sem = send_sem, recv_sem
        self.copies = []

    def send(self, src, dst, peer, at):
        copy = pltpu.make_async_remote_copy(
            src_ref=src,
            dst_ref=dst,
            send_sem=self.send_sem.at[at],
            recv_sem=self.recv_sem.at[at],
            device_id={"img": peer},
            device_id_type=MESH,
        )
        copy.start()
        self.copies.append(copy)

    def start(self, wide):
        for core in range(2):
            self.own[core] = wide[:, core]
        sibling = 1 - self.core
        self.send(self.own.at[sibling], self.other, self.chip * 2 + sibling, 0)
        return self

    def middle(self):
        self.copies[0].wait_recv()
        self.pair[...] = (self.own[self.core].astype(F32) + self.other[...].astype(F32)).astype(BF)
        self.landing[self.chip] = self.pair[self.chip]
        for step in range(1, self.chips):
            chip = lax.rem(self.chip + step, self.chips)
            self.send(self.pair.at[chip], self.landing.at[self.chip], chip * 2 + self.core, step)

    def result(self):
        for copy in self.copies[1:]:
            copy.wait_recv()
        return jnp.sum(self.landing[...].astype(F32), axis=0).astype(BF)

    def wait_send(self):
        for copy in self.copies:
            copy.wait_send()


def kernel(
    n_img, n_seq,
    pat_hbm, rou_hbm, win_hbm, wout_hbm, cot_hbm,
    left_hbm, right_hbm, rg_hbm, act_hbm, hg_hbm, in_hbm, gr_hbm,
    pat, rou, win, wout, cot,
    left, right, rg,
    a_in_s, a_in_r, a_gr_s, a_gr_r, a_st_s, a_st_r,
    b_in, b_gr, c_out, c_out_x, c_out_p, c_out_r, c_ig, c_ig_x, c_ig_p, c_ig_r,
    d_out, d_ig, d_st, e_s, e_r, f_buf, g_buf,
    act_s, hg_s,
    load_sem, store_sem, seq_send, seq_recv, img_send, img_recv, plane_send, plane_recv,
):
    img, seq = lax.axis_index("img"), lax.axis_index("seq")
    experts = win.shape[0]
    rows, depth = b_in.shape[1], b_in.shape[2]
    slots = n_seq * rows

    chips, chip, core = n_img // 2, img // 2, lax.rem(img, 2)

    def plane_peers():
        own = seq * 2 + core
        for step in range(1, n_seq * 2):
            peer = lax.rem(own + step, n_seq * 2)
            yield step, {"img": chip * 2 + lax.rem(peer, 2), "seq": peer // 2}, peer

    def chip_peers():
        for step in range(1, chips):
            yield step, {"img": lax.rem(chip + step, chips) * 2 + core}

    barrier = pltpu.get_barrier_semaphore()
    for _, device, _ in plane_peers():
        pl.semaphore_signal(barrier, inc=1, device_id=device, device_id_type=MESH)
    for _, device in chip_peers():
        pl.semaphore_signal(barrier, inc=1, device_id=device, device_id_type=MESH)

    loads = [
        pltpu.make_async_copy(src, dst, load_sem.at[at])
        for at, (src, dst) in enumerate(
            ((pat_hbm.at[0], pat), (rou_hbm, rou), (cot_hbm.at[0], cot), (win_hbm, win), (wout_hbm, wout))
        )
    ]
    for copy in loads[:3]:
        copy.start()

    def over_seq(at):
        return Exchange("seq", n_seq, seq_send.at[at], seq_recv.at[at])

    def relay(at, block):
        exchange = Relay(n_img, block, img_send.at[at], img_recv.at[at])
        started.append(exchange)
        return exchange.start()

    def pair_sum(at, wide, *buffers):
        exchange = PairSum(n_img, *buffers, img_send.at[at], img_recv.at[at])
        started.append(exchange)
        return exchange.start(wide)

    started = []

    def go(exchange, source, landing, own):
        exchange.start(source, landing, own)
        started.append(exchange)
        return exchange

    loads[1].wait()
    router_t = rou[...]
    loads[0].wait()
    logits = dot(router_t, pat[...], ((1,), (1,)))
    own_max = jnp.max(logits, axis=1, keepdims=True)
    raised = jnp.exp(logits - own_max)
    own_total = jnp.sum(raised, axis=1, keepdims=True)
    part_in = dot((raised * (1.0 / own_total)).astype(BF), pat[...], ((1,), (0,)))
    lane = lax.broadcasted_iota(jnp.int32, (slots, 128), 1)
    a_st_s[...] = jnp.where(lane == MAX_LANE, own_max, own_total).reshape(n_seq, rows, 128)
    a_in_s[...] = part_in.astype(BF).reshape(n_seq, rows, depth)
    a_st_r[seq] = a_st_s[seq]
    a_in_r[seq] = a_in_s[seq]
    pl.semaphore_wait(barrier, n_seq * 2 - 1 + chips - 1)
    a_st = go(over_seq(0), a_st_s, a_st_r, False)
    a_in = go(over_seq(1), a_in_s, a_in_r, False)
    for copy in loads[3:]:
        copy.start()

    comb = jnp.exp(logits - jnp.max(logits, axis=0, keepdims=True))
    comb = comb * (1.0 / jnp.sum(comb, axis=0, keepdims=True))
    loads[2].wait()
    part_gr = dot(comb.astype(BF), cot[...], ((1,), (0,)))
    a_gr_s[...] = part_gr.astype(BF).reshape(n_seq, rows, depth)
    a_gr_r[seq] = a_gr_s[seq]
    a_gr = go(over_seq(2), a_gr_s, a_gr_r, False)

    a_st.wait_recv()
    a_in.wait_recv()
    stats = a_st_r[...]
    maxes, totals = stats[:, :, MAX_LANE:MAX_LANE + 1], stats[:, :, TOTAL_LANE:TOTAL_LANE + 1]
    top = jnp.max(maxes, axis=0, keepdims=True)
    shares = totals * jnp.exp(maxes - top)
    total = jnp.sum(shares, axis=0, keepdims=True)
    slot_in = jnp.sum(a_in_r[...].astype(F32) * (shares / total), axis=0)
    b_in[img] = slot_in.astype(BF)
    g_in = relay(0, b_in)
    a_gr.wait_recv()
    b_gr[img] = jnp.sum(a_gr_r[...].astype(F32), axis=0).astype(BF)
    g_gr = relay(1, b_gr)

    def all_rows(parts):
        wide = [part.reshape(n_img, 1, SLOTS, depth) for part in parts]
        wide = jnp.concatenate(wide, axis=1).reshape(n_img // 2, 2, rows, depth)
        return wide.astype(BF)

    loads[3].wait()
    g_in.forward()
    g_gr.forward()
    g_in.wait_recv()
    slopes, parts = [], []
    loads[4].wait()
    for e in range(experts):
        hidden = dot(of_expert(b_in, e, experts), win[e], ((1,), (1,)))
        active, slope = gelu_and_slope(hidden)
        slopes.append(slope)
        act_s[e] = active.astype(BF)
        parts.append(dot(act_s[e], wout[e], ((1,), (0,))))
    out_sum = pair_sum(2, all_rows(parts), c_out, c_out_x, c_out_p, c_out_r)
    g_gr.wait_recv()
    parts = []
    for e in range(experts):
        act_grad = dot(of_expert(b_gr, e, experts), wout[e], ((1,), (1,)))
        hg_s[e] = (act_grad * slopes[e]).astype(BF)
        parts.append(dot(hg_s[e], win[e], ((1,), (0,))))
    ig_sum = pair_sum(3, all_rows(parts), c_ig, c_ig_x, c_ig_p, c_ig_r)
    out_sum.middle()
    ig_sum.middle()

    stores = []

    def store(src, dst):
        copy = pltpu.make_async_copy(src, dst, store_sem.at[len(stores)])
        copy.start()
        stores.append(copy)

    store(act_s, act_hbm)
    store(hg_s, hg_hbm)
    store(b_in, in_hbm)
    store(b_gr, gr_hbm)

    d_out[seq] = out_sum.result()
    e_out = go(over_seq(3), d_out, d_out, True)
    input_grad = ig_sum.result()
    d_ig[seq] = input_grad
    e_ig = go(over_seq(4), d_ig, d_ig, True)
    inner = jnp.sum(slot_in * input_grad.astype(F32), axis=1, keepdims=True)
    lane = lax.broadcasted_iota(jnp.int32, (rows, 128), 1)
    d_st[seq] = jnp.where(lane == MAX_LANE, top[0], jnp.where(lane == TOTAL_LANE, total[0], inner))
    e_st = go(over_seq(5), d_st, d_st, True)

    e_out.wait_recv()
    comb_grad = dot(d_out[...].reshape(slots, depth), cot[...], ((1,), (1,)))
    across = jnp.sum(comb * comb_grad, axis=0, keepdims=True)
    comb_part = comb * (comb_grad - across)
    e_ig.wait_recv()
    every_ig = d_ig[...].reshape(slots, depth)
    disp_grad = dot(every_ig, pat[...], ((1,), (1,)))
    e_st.wait_recv()
    stats = d_st[...].reshape(slots, 128)
    scale = jnp.exp(own_max - stats[:, MAX_LANE:MAX_LANE + 1]) / stats[:, TOTAL_LANE:TOTAL_LANE + 1]
    disp = raised * scale
    logit_grad = (disp * (disp_grad - stats[:, INNER_LANE:INNER_LANE + 1]) + comb_part).astype(BF)

    router_part = dot(logit_grad, pat[...], ((1,), (0,))).reshape(n_seq, rows, depth)
    half = depth // 2
    for side in range(2):
        e_s[:, side] = router_part[:, :, side * half:(side + 1) * half]
    e_r[seq * 2 + core] = e_s[seq, core]

    def to_plane(at, source, landing):
        copies = Copies(plane_send.at[at], plane_recv.at[at])
        for step, device, peer in plane_peers():
            copies.send(source(peer), landing, device, step)
        started.append(copies)
        return copies

    r_sum = to_plane(0, lambda peer: e_s.at[peer // 2, lax.rem(peer, 2)], e_r.at[seq * 2 + core])
    left[:slots] = logit_grad
    left[slots:] = disp.astype(BF)
    right[:slots] = router_t
    right[slots:] = every_ig
    store(left, left_hbm)
    store(right, right_hbm)
    r_sum.wait_recv()
    f_buf[chip] = jnp.sum(e_r[...], axis=0)
    r_all = Copies(img_send.at[4], img_recv.at[4])
    for step, device in chip_peers():
        r_all.send(f_buf.at[chip], f_buf.at[chip], device, step)
    started.append(r_all)
    r_all.wait_recv()
    own_block = g_buf.at[seq * 2 + core]
    own_block[...] = jnp.sum(f_buf[...], axis=0).astype(BF)
    to_plane(1, lambda peer: own_block, own_block).wait_recv()
    for at in range(n_seq):
        rg[at] = jnp.concatenate([g_buf[2 * at], g_buf[2 * at + 1]], axis=1)
    store(rg, rg_hbm)
    for exchange in started:
        exchange.wait_send()
    for copy in stores:
        copy.wait()


def write_kernel(
    left_hbm, right_hbm, rg_hbm, act_hbm, hg_hbm, in_hbm, gr_hbm,
    pg_out, rg_out, wig_out, wog_out,
    left, right, rg_in, act, hg, b_in, b_gr,
    pg, rg, wig, wog,
    load_sem, store_sem,
):
    experts, count = act.shape[0], left.shape[1]
    sources = (left_hbm, right_hbm, act_hbm, gr_hbm, hg_hbm, in_hbm, rg_hbm)
    loads = [
        pltpu.make_async_copy(src, dst, load_sem.at[at])
        for at, (src, dst) in enumerate(zip(sources, (left, right, act, b_gr, hg, b_in, rg_in)))
    ]
    for copy in loads:
        copy.start()
    stores = []

    def store(src, dst):
        copy = pltpu.make_async_copy(src, dst, store_sem.at[len(stores)])
        copy.start()
        stores.append(copy)

    loads[0].wait()
    loads[1].wait()
    for at in range(0, count, CHUNK):
        span = pl.ds(at, CHUNK)
        pg[span] = dot(left[:, span], right[...], ((0,), (0,))).astype(BF)
        store(pg.at[span], pg_out.at[0, span])
    loads[2].wait()
    loads[3].wait()
    for e in range(experts):
        wog[e] = dot(act[e], of_expert(b_gr, e, experts), ((0,), (0,))).astype(BF)
        store(wog.at[e], wog_out.at[e])
    loads[4].wait()
    loads[5].wait()
    for e in range(experts):
        wig[e] = dot(hg[e], of_expert(b_in, e, experts), ((0,), (0,))).astype(BF)
        store(wig.at[e], wig_out.at[e])
    loads[6].wait()
    rg[...] = rg_in[...].reshape(rg.shape)
    store(rg, rg_out)
    for copy in stores:
        copy.wait()


def local(n_img, n_seq, patches, router, w_in, w_out, cotangent):
    _, count, depth = patches.shape
    experts, units, _ = w_in.shape
    rows = experts * SLOTS
    slots = n_seq * rows
    by_unit = (experts, n_img * SLOTS, units)
    any_space = pl.BlockSpec(memory_space=pltpu.HBM)
    vmem = pltpu.VMEM
    by_seq, by_img = (n_seq, rows, depth), (n_img, rows, depth)
    by_chip, half = (n_img // 2, rows, depth), (rows, depth // 2)
    parts = pl.pallas_call(
        functools.partial(kernel, n_img, n_seq),
        out_shape=(
            jax.ShapeDtypeStruct((2 * slots, count), BF),
            jax.ShapeDtypeStruct((2 * slots, depth), BF),
            jax.ShapeDtypeStruct(by_seq, BF),
            jax.ShapeDtypeStruct(by_unit, BF),
            jax.ShapeDtypeStruct(by_unit, BF),
            jax.ShapeDtypeStruct(by_img, BF),
            jax.ShapeDtypeStruct(by_img, BF),
        ),
        in_specs=[any_space] * 5,
        out_specs=(any_space,) * 7,
        scratch_shapes=[
            vmem((count, depth), BF), vmem((slots, depth), BF), vmem(w_in.shape, BF),
            vmem(w_out.shape, BF), vmem((count, depth), BF),
            vmem((2 * slots, count), BF), vmem((2 * slots, depth), BF), vmem(by_seq, BF),
            vmem(by_seq, BF), vmem(by_seq, BF), vmem(by_seq, BF), vmem(by_seq, BF),
            vmem((n_seq, rows, 128), F32), vmem((n_seq, rows, 128), F32),
            vmem(by_img, BF), vmem(by_img, BF),
            vmem((2,) + by_chip, BF), vmem(by_chip, BF), vmem(by_chip, BF), vmem(by_chip, BF),
            vmem((2,) + by_chip, BF), vmem(by_chip, BF), vmem(by_chip, BF), vmem(by_chip, BF),
            vmem(by_seq, BF), vmem(by_seq, BF), vmem((n_seq, rows, 128), F32),
            vmem((n_seq, 2) + half, F32), vmem((n_seq * 2,) + half, F32),
            vmem((n_img // 2,) + half, F32), vmem((n_seq * 2,) + half, BF),
            vmem(by_unit, BF), vmem(by_unit, BF),
            pltpu.SemaphoreType.DMA((5,)), pltpu.SemaphoreType.DMA((7,)),
            pltpu.SemaphoreType.DMA((8, n_seq)), pltpu.SemaphoreType.DMA((8, n_seq)),
            pltpu.SemaphoreType.DMA((5, n_img)), pltpu.SemaphoreType.DMA((5, n_img)),
            pltpu.SemaphoreType.DMA((2, 2 * n_seq)), pltpu.SemaphoreType.DMA((2, 2 * n_seq)),
        ],
        compiler_params=pltpu.CompilerParams(
            collective_id=0, has_side_effects=True, vmem_limit_bytes=60 * 1024 * 1024
        ),
    )(patches, router.T, w_in, w_out, cotangent)
    patch_grad, router_grad, w_in_grad, w_out_grad = pl.pallas_call(
        write_kernel,
        out_shape=(
            jax.ShapeDtypeStruct(patches.shape, BF),
            jax.ShapeDtypeStruct((slots, depth), BF),
            jax.ShapeDtypeStruct(w_in.shape, BF),
            jax.ShapeDtypeStruct(w_out.shape, BF),
        ),
        in_specs=[any_space] * 7,
        out_specs=(any_space,) * 4,
        scratch_shapes=[
            vmem((2 * slots, count), BF), vmem((2 * slots, depth), BF), vmem(by_seq, BF),
            vmem(by_unit, BF), vmem(by_unit, BF), vmem(by_img, BF), vmem(by_img, BF),
            vmem((count, depth), BF), vmem((slots, depth), BF), vmem(w_in.shape, BF), vmem(w_out.shape, BF),
            pltpu.SemaphoreType.DMA((7,)), pltpu.SemaphoreType.DMA((3 + 2 * experts + count // CHUNK,)),
        ],
        compiler_params=pltpu.CompilerParams(vmem_limit_bytes=60 * 1024 * 1024),
    )(*parts)
    return patch_grad, router_grad.T, w_in_grad, w_out_grad


def solution(mesh):
    placed = (
        P("img", "seq", None),
        P(),
        P("seq", "img", None),
        P("seq", "img", None),
        P("img", "seq", None),
    )
    return jax.shard_map(
        functools.partial(local, mesh.shape["img"], mesh.shape["seq"]),
        mesh=mesh,
        in_specs=placed,
        out_specs=(P("img", "seq", None), P(), P("seq", "img", None), P("seq", "img", None)),
        check_vma=False,
    )
```
